32 devices in a mesh: dp: 2 (over y), row: 4 (over z), col: 4 (over x, core).
Axes of the slice: x: 2, y: 2, z: 4, core: 2. Of those that a mesh axis runs over, the one named last changes fastest.
Arguments:
- images_in: bfloat16 [8, 64, 64, 1024], P('dp', 'row', 'col'), may hold values from -6 to 6
- keep: int32 [8], P('dp'), may hold values from 0 to 1, as said below
- dw_weight: bfloat16 [49, 1024], replicated, may hold values from -0.875 to 0.875
- layer_norm_gain: float32 [1024], replicated, may hold values from 0.25 to 1.75
- w_in: bfloat16 [1024, 2048], replicated, may hold values from -0.1875 to 0.1875
- w_out: bfloat16 [2048, 1024], replicated, may hold values from -0.125 to 0.125
- layer_scale: float32 [1024], replicated, may hold values from 0.25 to 1
- out_grad: bfloat16 [8, 64, 64, 1024], P('dp', 'row', 'col'), may hold values from -6 to 6
Outputs:
- output: bfloat16 [8, 64, 64, 1024], P('dp', 'row', 'col')
- grad_input: bfloat16 [8, 64, 64, 1024], P('dp', 'row', 'col')
- grad_w_in: float32 [1024, 2048], P(('dp', 'row', 'col'))
- grad_w_out: float32 [2048, 1024], P(('dp', 'row', 'col'))
- grad_dw: float32 [49, 1024], replicated
- grad_ln_gain: float32 [1024], replicated
- grad_layer_scale: float32 [1024], replicated
The draws below stay inside these ranges and needn't reach their ends.
Inputs may be any that keep to these rules, and one draw needn't show every extreme that they name: `keep`: 1 keeps the image's residual branch, 0 drops it; at least one and at most 4 images are dropped.
All inputs are finite; a program needn't handle non-finite values.
Results may differ from the reference program's by a relative error of at most 0.0062.
Values may be sent and summed in bfloat16 or wider, within the bound.
A program may use at most 128 MiB of HBM per device.

```python
import math
import jax
import jax.numpy as jnp
from jax import lax

C = 1024
HID = 2048
KERNEL = 7
MAP = 64
IMAGES = 8


def draw_keep(key, part):
    order_key = jax.random.fold_in(key, 11)
    count_key = jax.random.fold_in(key, 23)
    order = jax.random.permutation(order_key, IMAGES).astype(jnp.int32)
    dropped = jax.random.randint(count_key, (), 1, IMAGES // 2 + 1).astype(jnp.int32)
    return (order >= dropped).astype(jnp.int32)


def block_levels(own_key, dims, pieces, low, top_value):
    gain, own = 1.0, jax.random.fold_in(own_key, 6)
    for axis_at, parts in pieces:
        heights = jnp.exp(jax.random.uniform(jax.random.fold_in(own, axis_at), (parts,), jnp.float32, low / len(pieces), top_value / len(pieces)))
        gain = gain * jnp.repeat(heights, dims[axis_at] // parts).reshape([-1 if axis == axis_at else 1 for axis in range(len(dims))])
    return gain


def centred(key, dims, deviation, limit, split=(), kind=jnp.bfloat16):
    gain = block_levels(key, dims, split, -0.22, 0.18) if split else 1.0
    values = jax.random.normal(key, dims, jnp.float32) * deviation * gain
    return jnp.minimum(jnp.maximum(values, -limit), limit).astype(kind)


def setup_inputs(seed: int = 0) -> dict:
    splits = jax.random.split(jax.random.key(seed), 9)
    images_in = centred(splits[0], (IMAGES, MAP, MAP, C), 1.0, 6.0, ((0, 2), (1, 4), (2, 4)))
    keep = draw_keep(jax.random.fold_in(splits[8], 71), 0)
    dw_weight = centred(splits[2], (KERNEL * KERNEL, C), (KERNEL * KERNEL) ** -0.5, 0.875)
    layer_norm_gain = jnp.clip(1.0 + 0.15 * jax.random.normal(splits[3], (C,), jnp.float32), 0.25, 1.75)
    w_in = centred(splits[4], (C, HID), C ** -0.5, 0.1875)
    w_out = centred(splits[5], (HID, C), HID ** -0.5, 0.125)
    layer_scale = jnp.clip(jnp.exp(jax.random.uniform(splits[6], (C,), jnp.float32, math.log(0.25), math.log(1.0))), 0.25, 1.0)
    out_grad = centred(splits[7], (IMAGES, MAP, MAP, C), 1.0, 6.0, ((0, 2), (1, 4), (2, 4)))
    return {"images_in": images_in, "keep": keep, "dw_weight": dw_weight, "layer_norm_gain": layer_norm_gain, "w_in": w_in, "w_out": w_out, "layer_scale": layer_scale, "out_grad": out_grad}


eps = 1e-06
keep_rate = 0.75

def depthwise(padded, kernel, width):
    taps = kernel.reshape(KERNEL, KERNEL, 1, width)
    return lax.conv_general_dilated(padded, taps, (1, 1), 'VALID', dimension_numbers=('NHWC', 'HWIO', 'NHWC'), feature_group_count=width, preferred_element_type=jnp.float32)

def reference(images_in, keep, dw_weight, layer_norm_gain, w_in, w_out, layer_scale, out_grad):
    rim = KERNEL // 2
    flipped = dw_weight.reshape(KERNEL, KERNEL, C)[::-1, ::-1].reshape(KERNEL * KERNEL, C)

    def one(carry, items):
        image, kept, upstream_in = items
        padded = jnp.pad(image, ((rim, rim), (rim, rim), (0, 0)))[None]
        conv = depthwise(padded, dw_weight, C)[0].reshape(MAP * MAP, C)
        mean_v = lax.optimization_barrier(jnp.mean(conv, axis=-1, keepdims=True))
        local_device = conv - mean_v
        inverse_deviation = lax.rsqrt(lax.optimization_barrier(jnp.mean(local_device * local_device, axis=-1, keepdims=True)) + eps)
        centered_scaled_input = local_device * inverse_deviation
        normalized_input = (centered_scaled_input * layer_norm_gain).astype(jnp.bfloat16)
        pre = jnp.dot(normalized_input, w_in, preferred_element_type=jnp.float32)
        cdf = 0.5 * (1.0 + lax.erf(pre * (1.0 / math.sqrt(2.0))))
        hidden = (pre * cdf).astype(jnp.bfloat16)
        branch = jnp.dot(hidden, w_out, preferred_element_type=jnp.float32)
        factor = kept.astype(jnp.float32) / keep_rate
        flat_in = image.reshape(MAP * MAP, C).astype(jnp.float32)
        output = (flat_in + factor * layer_scale * branch).astype(jnp.bfloat16)
        upstream = upstream_in.reshape(MAP * MAP, C).astype(jnp.float32)
        g_branch = (factor * layer_scale * upstream).astype(jnp.bfloat16)
        gamma_term = lax.optimization_barrier(jnp.sum(factor * upstream * branch, axis=0))
        slope = cdf + pre * jnp.exp(-0.5 * pre * pre) * (1.0 / math.sqrt(2.0 * math.pi))
        g_pre = (jnp.dot(g_branch, w_out.T, preferred_element_type=jnp.float32) * slope).astype(jnp.bfloat16)
        normalized_gradient = jnp.dot(g_pre, w_in.T, preferred_element_type=jnp.float32)
        gain_contribution = lax.optimization_barrier(jnp.sum(normalized_gradient * centered_scaled_input, axis=0))
        input_gradient = normalized_gradient * layer_norm_gain
        convolution_gradient = (inverse_deviation * (input_gradient - lax.optimization_barrier(jnp.mean(input_gradient, axis=-1, keepdims=True)) - centered_scaled_input * lax.optimization_barrier(jnp.mean(input_gradient * centered_scaled_input, axis=-1, keepdims=True)))).astype(jnp.bfloat16)
        g_conv3 = convolution_gradient.reshape(MAP, MAP, C)
        g_wide = g_conv3.astype(jnp.float32)
        dw_terms = []
        for i in range(KERNEL):
            for j in range(KERNEL):
                window = padded[0, i:i + MAP, j:j + MAP, :].astype(jnp.float32)
                dw_terms.append(lax.optimization_barrier(jnp.sum(g_wide * window, axis=(0, 1))))
        dw_term = jnp.stack(dw_terms, axis=0)
        g_padded = jnp.pad(g_conv3, ((rim, rim), (rim, rim), (0, 0)))[None]
        back = depthwise(g_padded, flipped, C)[0].reshape(MAP * MAP, C)
        grad_in = (upstream + back).astype(jnp.bfloat16)
        w_in_term = jnp.dot(normalized_input.T, g_pre, preferred_element_type=jnp.float32)
        w_out_term = jnp.dot(hidden.T, g_branch, preferred_element_type=jnp.float32)
        total_in, total_out, total_dw, total_gain, total_gamma = carry
        carry = (total_in + w_in_term, total_out + w_out_term, total_dw + dw_term, total_gain + gain_contribution, total_gamma + gamma_term)
        return (carry, (output.reshape(MAP, MAP, C), grad_in.reshape(MAP, MAP, C)))
    start = (jnp.zeros((C, HID), jnp.float32), jnp.zeros((HID, C), jnp.float32), jnp.zeros((KERNEL * KERNEL, C), jnp.float32), jnp.zeros((C,), jnp.float32), jnp.zeros((C,), jnp.float32))
    totals, stacked = lax.scan(one, start, (images_in, keep, out_grad))
    count = jnp.float32(IMAGES)
    return (stacked[0], stacked[1], totals[0] / count, totals[1] / count, totals[2] / count, totals[3] / count, totals[4] / count)
```

```python
import math

import jax
import jax.numpy as jnp
from jax import lax
from jax.experimental import pallas as pl
from jax.experimental.pallas import tpu as pltpu
from jax.sharding import PartitionSpec as P

KERNEL = 7


eps = 1e-06
keep_rate = 0.75


def extended(block, sides, width):
    for axis, dim in sides:
        count = lax.axis_size(axis)
        forward = [(i, i + 1) for i in range(count - 1)]
        backward = [(target, source) for source, target in forward]
        low = lax.ppermute(
            lax.slice_in_dim(block, block.shape[dim] - width, None, axis=dim), axis, forward
        )
        high = lax.ppermute(lax.slice_in_dim(block, 0, width, axis=dim), axis, backward)
        block = jnp.concatenate([low, block, high], axis=dim)
    return block


LANES = 128


def shifted_views(source, views, tile_w):
    wide = source[0].astype(jnp.float32)
    for j in range(KERNEL):
        views[j] = wide[:, j : j + tile_w, :]


def conv_kernel(x_ref, w_ref, *rest):
    extra, o_ref, views = (rest[0] if len(rest) == 3 else None), rest[-2], rest[-1]
    tile_h, tile_w = o_ref.shape[1], o_ref.shape[2]
    shifted_views(x_ref, views, tile_w)
    half = tile_h // 2
    for top in range(0, tile_h, half):
        acc = jnp.zeros((half, tile_w, LANES), jnp.float32)
        for i in range(KERNEL):
            for j in range(KERNEL):
                tap = i * KERNEL + j
                weight = w_ref[tap : tap + 1, :][None]
                acc = acc + views[j, top + i : top + i + half] * weight
        if extra is not None:
            acc = acc + extra[0, top : top + half].astype(jnp.float32)
        o_ref[0, top : top + half] = acc.astype(o_ref.dtype)


def depthwise(padded, weights, extra, dtype):
    batch, full_h, full_w, width = padded.shape
    tile_h, tile_w = full_h - KERNEL + 1, full_w - KERNEL + 1
    cell_spec = pl.BlockSpec((1, tile_h, tile_w, LANES), lambda c, n: (n, 0, 0, c))
    in_specs = [
        pl.BlockSpec((1, full_h, full_w, LANES), lambda c, n: (n, 0, 0, c)),
        pl.BlockSpec((KERNEL * KERNEL, LANES), lambda c, n: (0, c)),
    ]
    operands = [padded, weights.astype(jnp.float32)]
    if extra is not None:
        in_specs.append(cell_spec)
        operands.append(extra)
    size = batch * tile_h * tile_w * width
    return pl.pallas_call(
        conv_kernel,
        grid=(width // LANES, batch),
        in_specs=in_specs,
        out_specs=cell_spec,
        out_shape=jax.ShapeDtypeStruct((batch, tile_h, tile_w, width), dtype),
        scratch_shapes=[pltpu.VMEM((KERNEL, full_h, tile_w, LANES), jnp.float32)],
        compiler_params=pltpu.CompilerParams(vmem_limit_bytes=24 * 2**20),
        cost_estimate=pl.CostEstimate(flops=98 * size * 150, bytes_accessed=6 * size, transcendentals=0),
    )(*operands)


def dw_kernel(x_ref, g_ref, o_ref, views, total):
    step = pl.program_id(1)
    tile_h, tile_w = g_ref.shape[1], g_ref.shape[2]
    shifted_views(x_ref, views, tile_w)

    @pl.when(step == 0)
    def _():
        total[...] = jnp.zeros_like(total)

    half = tile_h // 2
    for top in range(0, tile_h, half):
        g = g_ref[0, top : top + half].astype(jnp.float32)
        for i in range(KERNEL):
            for j in range(KERNEL):
                part = jnp.sum(views[j, top + i : top + i + half] * g, axis=0)
                part = jnp.sum(part.reshape(tile_w // 8, 8, LANES), axis=0)
                total[i * KERNEL + j] += part

    @pl.when(step == pl.num_programs(1) - 1)
    def _():
        o_ref[...] = jnp.sum(total[...], axis=1)


def kernel_gradient(padded, g_conv):
    batch, full_h, full_w, width = padded.shape
    tile_h, tile_w = full_h - KERNEL + 1, full_w - KERNEL + 1
    size = batch * tile_h * tile_w * width
    return pl.pallas_call(
        dw_kernel,
        grid=(width // LANES, batch),
        in_specs=[
            pl.BlockSpec((1, full_h, full_w, LANES), lambda c, n: (n, 0, 0, c)),
            pl.BlockSpec((1, tile_h, tile_w, LANES), lambda c, n: (n, 0, 0, c)),
        ],
        out_specs=pl.BlockSpec((KERNEL * KERNEL, LANES), lambda c, n: (0, c)),
        out_shape=jax.ShapeDtypeStruct((KERNEL * KERNEL, width), jnp.float32),
        scratch_shapes=[
            pltpu.VMEM((KERNEL, full_h, tile_w, LANES), jnp.float32),
            pltpu.VMEM((KERNEL * KERNEL, 8, LANES), jnp.float32),
        ],
        compiler_params=pltpu.CompilerParams(vmem_limit_bytes=24 * 2**20),
        cost_estimate=pl.CostEstimate(flops=98 * size * 150, bytes_accessed=6 * size, transcendentals=0),
    )(padded, g_conv)


def halved(term, order):
    names = ("dp", "row", "col")
    sizes = [lax.axis_size(name) for name in names]
    devices = math.prod(sizes)
    rows = term.shape[0] // devices
    part = term.reshape(*sizes, rows, term.shape[1])
    done = {name: 0 for name in names}
    for name in order:
        dim, count = names.index(name), lax.axis_size(name)
        stride = 2 ** done[name]
        done[name] += 1
        index = lax.axis_index(name)
        bit = (index // stride) % 2
        left = part.shape[dim]
        shape = part.shape[:dim] + (left // 2, 2) + part.shape[dim + 1 :]
        pairs = part.reshape(shape)
        mine = lax.dynamic_index_in_dim(pairs, bit, dim + 1, keepdims=False)
        theirs = lax.dynamic_index_in_dim(pairs, 1 - bit, dim + 1, keepdims=False)
        swap = [(k, k ^ stride) for k in range(count)]
        got = lax.ppermute(theirs.astype(jnp.bfloat16), name, swap)
        part = mine.astype(jnp.float32) + got.astype(jnp.float32)
        if sum(done.values()) < len(order):
            part = part.astype(jnp.bfloat16)
    return part.reshape(rows, term.shape[1])


def steps_of(*names):
    bits = {name: int(math.log2(lax.axis_size(name))) for name in names}
    bits["col"] -= 1
    order = ["col"]
    for name in names:
        order += [name] * bits[name]
    return order


def extend(field):
    return extended(field, (("row", 1), ("col", 2)), KERNEL // 2)


def shards(images_in, keep, dw_weight, layer_norm_gain, w_in, w_out, layer_scale, out_grad):
    batch, tile_h, tile_w, width = images_in.shape
    cells = tile_h * tile_w
    total_rows = batch * cells
    padded = extend(images_in)
    conv = depthwise(padded, dw_weight, None, jnp.float32).reshape(total_rows, width)
    mean_v = jnp.mean(conv, axis=-1, keepdims=True)
    local_device = conv - mean_v
    inverse_deviation = lax.rsqrt(
        jnp.mean(local_device * local_device, axis=-1, keepdims=True) + eps
    )
    centered_scaled_input = local_device * inverse_deviation
    normalized_input = (centered_scaled_input * layer_norm_gain).astype(jnp.bfloat16)
    pre = jnp.dot(normalized_input, w_in, preferred_element_type=jnp.float32)
    cdf = 0.5 * (1.0 + lax.erf(pre * (1.0 / math.sqrt(2.0))))
    hidden = (pre * cdf).astype(jnp.bfloat16)
    branch = jnp.dot(hidden, w_out, preferred_element_type=jnp.float32)
    factor = jnp.repeat(keep.astype(jnp.float32) / keep_rate, cells)[:, None]
    flat_in = images_in.reshape(total_rows, width).astype(jnp.float32)
    output = (flat_in + factor * layer_scale * branch).astype(jnp.bfloat16).reshape(images_in.shape)
    upstream = out_grad.reshape(total_rows, width).astype(jnp.float32)
    g_branch = (factor * layer_scale * upstream).astype(jnp.bfloat16)
    gamma_term = jnp.sum(factor * upstream * branch, axis=0)
    slope = cdf + pre * jnp.exp(-0.5 * pre * pre) * (1.0 / math.sqrt(2.0 * math.pi))
    g_pre = (jnp.dot(g_branch, w_out.T, preferred_element_type=jnp.float32) * slope).astype(
        jnp.bfloat16
    )
    normalized_gradient = jnp.dot(g_pre, w_in.T, preferred_element_type=jnp.float32)
    gain_contribution = jnp.sum(normalized_gradient * centered_scaled_input, axis=0)
    input_gradient = normalized_gradient * layer_norm_gain
    convolution_gradient = (
        inverse_deviation
        * (
            input_gradient
            - jnp.mean(input_gradient, axis=-1, keepdims=True)
            - centered_scaled_input
            * jnp.mean(input_gradient * centered_scaled_input, axis=-1, keepdims=True)
        )
    ).astype(jnp.bfloat16)
    g_conv4 = convolution_gradient.reshape(batch, tile_h, tile_w, width)
    dw_term = kernel_gradient(padded, g_conv4)
    flipped = dw_weight.reshape(KERNEL, KERNEL, width)[::-1, ::-1].reshape(KERNEL * KERNEL, width)
    grad_input = depthwise(extend(g_conv4), flipped, out_grad, jnp.bfloat16)
    images = jnp.float32(batch * lax.axis_size("dp"))
    small = jnp.concatenate([dw_term, gain_contribution[None], gamma_term[None]], axis=0)
    small = lax.psum(small, ("dp", "row", "col")) / images
    taps = KERNEL * KERNEL
    dw_sum, gain_sum, gamma_sum = small[:taps], small[taps], small[taps + 1]
    w_out_term = jnp.dot(hidden.T, g_branch, preferred_element_type=jnp.float32).astype(jnp.bfloat16)
    w_in_term = jnp.dot(normalized_input.T, g_pre, preferred_element_type=jnp.float32).astype(jnp.bfloat16)
    w_out_sum = halved(w_out_term, steps_of("col", "row", "dp"))
    w_in_sum = halved(w_in_term, steps_of("dp", "row", "col"))
    return (
        output,
        grad_input,
        w_in_sum / images,
        w_out_sum / images,
        dw_sum,
        gain_sum,
        gamma_sum,
    )


def solution(mesh):
    placed = (
        P("dp", "row", "col", None),
        P("dp"),
        P(),
        P(),
        P(),
        P(),
        P(),
        P("dp", "row", "col", None),
    )
    return jax.shard_map(
        shards,
        mesh=mesh,
        in_specs=placed,
        out_specs=(
            P("dp", "row", "col", None),
            P("dp", "row", "col", None),
            P(("dp", "row", "col"), None),
            P(("dp", "row", "col"), None),
            P(),
            P(),
            P(),
        ),
        check_vma=False,
    )
```

```python
import math

import jax
import jax.numpy as jnp
from jax import lax
from jax.experimental import pallas as pl
from jax.experimental.pallas import tpu as pltpu
from jax.sharding import PartitionSpec as P

KERNEL = 7


eps = 1e-06
keep_rate = 0.75


def extend(field, width=KERNEL // 2):
    rows, cols = lax.axis_size("row"), lax.axis_size("col")
    pieces = []
    for down in (-1, 0, 1):
        line = []
        for right in (-1, 0, 1):
            if down == 0 and right == 0:
                line.append(field)
                continue
            part = field
            for step, dim in ((down, 1), (right, 2)):
                full = field.shape[dim]
                if step == -1:
                    part = lax.slice_in_dim(part, full - width, None, axis=dim)
                elif step == 1:
                    part = lax.slice_in_dim(part, 0, width, axis=dim)
            pairs = []
            for r in range(rows):
                for c in range(cols):
                    if 0 <= r + down < rows and 0 <= c + right < cols:
                        pairs.append(((r + down) * cols + c + right, r * cols + c))
            line.append(lax.ppermute(part, ("row", "col"), pairs))
        pieces.append(line)
    return jnp.concatenate([jnp.concatenate(line, axis=2) for line in pieces], axis=1)


def extend_along(field, axis, dim, width=KERNEL // 2):
    forward = [(k, k + 1) for k in range(lax.axis_size(axis) - 1)]
    backward = [(target, source) for source, target in forward]
    full = field.shape[dim]
    low = lax.ppermute(lax.slice_in_dim(field, full - width, None, axis=dim), axis, forward)
    high = lax.ppermute(lax.slice_in_dim(field, 0, width, axis=dim), axis, backward)
    return jnp.concatenate([low, field, high], axis=dim)


def after(value, *others):
    return lax.optimization_barrier((value, *others))[0]


LANES = 128


def shifted_views(source, views, tile_w):
    wide = source[0].astype(jnp.float32)
    for j in range(KERNEL):
        views[j] = wide[:, j : j + tile_w, :]


def taps_sum(views, w_ref, top, rows, tile_w):
    acc = jnp.zeros((rows, tile_w, LANES), jnp.float32)
    for i in range(KERNEL):
        for j in range(KERNEL):
            tap = i * KERNEL + j
            acc = acc + views[j, top + i : top + i + rows] * w_ref[tap : tap + 1, :][None]
    return acc


def norm_kernel(x_ref, w_ref, gain_ref, xhat_ref, normed_ref, rstd_ref, views, held):
    step = pl.program_id(1)
    tile_h, tile_w, width = xhat_ref.shape[1:]
    shifted_views(x_ref, views, tile_w)
    half = tile_h // 2
    for top in range(0, tile_h, half):
        held[step, top : top + half] = taps_sum(views, w_ref, top, half, tile_w)

    @pl.when(step == pl.num_programs(1) - 1)
    def _():
        blocks = width // LANES

        @pl.loop(0, tile_h)
        def _(row):
            conv = [held[block, row] for block in range(blocks)]
            mean = jnp.sum(sum(conv), axis=-1, keepdims=True) / width
            centred = [part - mean for part in conv]
            spread = jnp.sum(sum(part * part for part in centred), axis=-1, keepdims=True)
            rstd = lax.rsqrt(spread / width + eps)
            rstd_ref[0, row] = rstd
            for block in range(blocks):
                lanes = slice(block * LANES, (block + 1) * LANES)
                xhat = centred[block] * rstd
                xhat_ref[0, row, :, lanes] = xhat
                normed_ref[0, row, :, lanes] = (xhat * gain_ref[:, lanes]).astype(jnp.bfloat16)


def conv_norm(padded, weights, gain):
    batch, full_h, full_w, width = padded.shape
    tile_h, tile_w = full_h - KERNEL + 1, full_w - KERNEL + 1
    size = batch * tile_h * tile_w * width
    shape = (batch, tile_h, tile_w, width)
    whole = pl.BlockSpec((1, tile_h, tile_w, width), lambda n, c: (n, 0, 0, 0))
    return pl.pallas_call(
        norm_kernel,
        grid=(batch, width // LANES),
        in_specs=[
            pl.BlockSpec((1, full_h, full_w, LANES), lambda n, c: (n, 0, 0, c)),
            pl.BlockSpec((KERNEL * KERNEL, LANES), lambda n, c: (0, c)),
            pl.BlockSpec((1, width), lambda n, c: (0, 0)),
        ],
        out_specs=[whole, whole, pl.BlockSpec((1, tile_h, tile_w, 1), lambda n, c: (n, 0, 0, 0))],
        out_shape=[
            jax.ShapeDtypeStruct(shape, jnp.float32),
            jax.ShapeDtypeStruct(shape, jnp.bfloat16),
            jax.ShapeDtypeStruct(shape[:3] + (1,), jnp.float32),
        ],
        scratch_shapes=[
            pltpu.VMEM((KERNEL, full_h, tile_w, LANES), jnp.float32),
            pltpu.VMEM((width // LANES, tile_h, tile_w, LANES), jnp.float32),
        ],
        compiler_params=pltpu.CompilerParams(vmem_limit_bytes=24 * 2**20),
        cost_estimate=pl.CostEstimate(flops=15000 * size, bytes_accessed=8 * size, transcendentals=0),
    )(padded, weights.astype(jnp.float32), gain[None])


def back_kernel(x_ref, w_ref, extra_ref, *rest):
    o_ref, views = rest[-2:]
    tile_h, tile_w = o_ref.shape[1], o_ref.shape[2]
    shifted_views(x_ref, views, tile_w)
    half = tile_h // 2
    for top in range(0, tile_h, half):
        acc = taps_sum(views, w_ref, top, half, tile_w)
        acc = acc + extra_ref[0, top : top + half].astype(jnp.float32)
        o_ref[0, top : top + half] = acc.astype(o_ref.dtype)


def conv_back(padded, weights, extra, start, count, earlier):
    batch, full_h, full_w, width = padded.shape
    tile_h, tile_w = full_h - KERNEL + 1, full_w - KERNEL + 1
    cell_spec = pl.BlockSpec((1, tile_h, tile_w, LANES), lambda c, n: (n + start, 0, 0, c))
    in_specs = [
        pl.BlockSpec((1, full_h, full_w, LANES), lambda c, n: (n + start, 0, 0, c)),
        pl.BlockSpec((KERNEL * KERNEL, LANES), lambda c, n: (0, c)),
        cell_spec,
    ]
    operands, aliases = [padded, weights.astype(jnp.float32), extra], {}
    if earlier is not None:
        in_specs.append(pl.BlockSpec(memory_space=pl.ANY))
        operands.append(earlier)
        aliases = {3: 0}
    size = count * tile_h * tile_w * width
    return pl.pallas_call(
        back_kernel,
        grid=(width // LANES, count),
        in_specs=in_specs,
        out_specs=cell_spec,
        out_shape=jax.ShapeDtypeStruct((batch, tile_h, tile_w, width), jnp.bfloat16),
        input_output_aliases=aliases,
        scratch_shapes=[pltpu.VMEM((KERNEL, full_h, tile_w, LANES), jnp.float32)],
        compiler_params=pltpu.CompilerParams(vmem_limit_bytes=24 * 2**20),
        cost_estimate=pl.CostEstimate(flops=15000 * size, bytes_accessed=6 * size, transcendentals=0),
    )(*operands)


def dw_kernel(x_ref, g_ref, o_ref, views, total):
    step = pl.program_id(1)
    tile_h, tile_w = g_ref.shape[1], g_ref.shape[2]
    shifted_views(x_ref, views, tile_w)

    @pl.when(step == 0)
    def _():
        total[...] = jnp.zeros_like(total)

    half = tile_h // 2
    for top in range(0, tile_h, half):
        g = g_ref[0, top : top + half].astype(jnp.float32)
        for i in range(KERNEL):
            for j in range(KERNEL):
                part = jnp.sum(views[j, top + i : top + i + half] * g, axis=0)
                part = jnp.sum(part.reshape(tile_w // 8, 8, LANES), axis=0)
                total[i * KERNEL + j] += part

    @pl.when(step == pl.num_programs(1) - 1)
    def _():
        o_ref[...] = jnp.sum(total[...], axis=1)


def kernel_gradient(padded, g_conv, part, parts):
    batch, full_h, full_w, width = padded.shape
    tile_h, tile_w = full_h - KERNEL + 1, full_w - KERNEL + 1
    blocks = width // LANES // parts
    start = blocks * part
    size = batch * tile_h * tile_w * blocks * LANES
    return pl.pallas_call(
        dw_kernel,
        grid=(blocks, batch),
        in_specs=[
            pl.BlockSpec((1, full_h, full_w, LANES), lambda c, n: (n, 0, 0, c + start)),
            pl.BlockSpec((1, tile_h, tile_w, LANES), lambda c, n: (n, 0, 0, c + start)),
        ],
        out_specs=pl.BlockSpec((KERNEL * KERNEL, LANES), lambda c, n: (0, c)),
        out_shape=jax.ShapeDtypeStruct((KERNEL * KERNEL, blocks * LANES), jnp.float32),
        scratch_shapes=[
            pltpu.VMEM((KERNEL, full_h, tile_w, LANES), jnp.float32),
            pltpu.VMEM((KERNEL * KERNEL, 8, LANES), jnp.float32),
        ],
        compiler_params=pltpu.CompilerParams(vmem_limit_bytes=24 * 2**20),
        cost_estimate=pl.CostEstimate(flops=15000 * size, bytes_accessed=6 * size, transcendentals=0),
    )(padded, g_conv)


class Halving:
    def __init__(self, term, order):
        names = ("dp", "row", "col")
        sizes = [lax.axis_size(name) for name in names]
        self.names, self.order = names, list(order)
        self.rows, self.columns = term.shape[0] // math.prod(sizes), term.shape[1]
        self.part = term.reshape(*sizes, self.rows, self.columns)
        self.done = {name: 0 for name in names}

    def step(self):
        name = self.order.pop(0)
        dim, count = self.names.index(name), lax.axis_size(name)
        stride = 2 ** self.done[name]
        self.done[name] += 1
        bit = (lax.axis_index(name) // stride) % 2
        part = self.part
        left = part.shape[dim]
        pairs = part.reshape(part.shape[:dim] + (left // 2, 2) + part.shape[dim + 1 :])
        mine = lax.dynamic_index_in_dim(pairs, bit, dim + 1, keepdims=False)
        theirs = lax.dynamic_index_in_dim(pairs, 1 - bit, dim + 1, keepdims=False)
        swap = [(k, k ^ stride) for k in range(count)]
        got = lax.ppermute(theirs.astype(jnp.bfloat16), name, swap)
        part = mine.astype(jnp.float32) + got.astype(jnp.float32)
        self.part = part.astype(jnp.bfloat16) if self.order else part
        return self.part

    def finish(self):
        while self.order:
            self.step()
        return self.part.reshape(self.rows, self.columns)


def rotated(value, axis, shift):
    count = lax.axis_size(axis)
    return lax.ppermute(value, axis, [(k, (k + shift) % count) for k in range(count)])


def scatter_sum(rows, axis):
    count, me = lax.axis_size(axis), lax.axis_index(axis)
    shares = rows.reshape(count, rows.shape[0] // count, rows.shape[1])
    total = lax.dynamic_index_in_dim(shares, me, 0, keepdims=False)
    for shift in range(1, count):
        away = lax.dynamic_index_in_dim(shares, (me + shift) % count, 0, keepdims=False)
        total = total + rotated(away, axis, shift)
    return total


def ordered_sum(rows, axis):
    shares = collected(rows, axis)
    total = shares[0]
    for share in shares[1:]:
        total = total + share
    return total


def collected(rows, axis):
    count, me = lax.axis_size(axis), lax.axis_index(axis)
    came = jnp.stack([rows] + [rotated(rows, axis, shift) for shift in range(1, count)])
    return [
        lax.dynamic_index_in_dim(came, (me - k) % count, 0, keepdims=False) for k in range(count)
    ]


def steps_of(*names):
    bits = {name: int(math.log2(lax.axis_size(name))) for name in names}
    bits["col"] -= 1
    order = ["col"]
    for name in names:
        order += [name] * bits[name]
    return order


def shards(images_in, keep, dw_weight, layer_norm_gain, w_in, w_out, layer_scale, out_grad):
    batch, tile_h, tile_w, width = images_in.shape
    cells = tile_h * tile_w
    total_rows = batch * cells
    padded = extend(images_in)
    xhat, normed, rstd = conv_norm(padded, dw_weight, layer_norm_gain)
    centered_scaled_input = xhat.reshape(total_rows, width)
    normalized_input = normed.reshape(total_rows, width)
    inverse_deviation = rstd.reshape(total_rows, 1)
    pre = jnp.dot(normalized_input, w_in, preferred_element_type=jnp.float32)
    cdf = 0.5 * (1.0 + lax.erf(pre * (1.0 / math.sqrt(2.0))))
    hidden = (pre * cdf).astype(jnp.bfloat16)
    branch = jnp.dot(hidden, w_out, preferred_element_type=jnp.float32)
    factor = jnp.repeat(keep.astype(jnp.float32) / keep_rate, cells)[:, None]
    flat_in = images_in.reshape(total_rows, width).astype(jnp.float32)
    output = (flat_in + factor * layer_scale * branch).astype(jnp.bfloat16).reshape(images_in.shape)
    upstream = out_grad.reshape(total_rows, width).astype(jnp.float32)
    g_branch = (factor * layer_scale * upstream).astype(jnp.bfloat16)
    w_out_term = jnp.dot(hidden.T, g_branch, preferred_element_type=jnp.float32).astype(jnp.bfloat16)
    w_out_share = Halving(w_out_term, steps_of("col", "row", "dp"))
    gamma_term = jnp.sum(factor * upstream * branch, axis=0)
    slope = cdf + pre * jnp.exp(-0.5 * pre * pre) * (1.0 / math.sqrt(2.0 * math.pi))
    g_pre = (jnp.dot(after(g_branch, w_out_term), w_out.T, preferred_element_type=jnp.float32) * slope).astype(
        jnp.bfloat16
    )
    normalized_gradient = jnp.dot(after(g_pre, w_out_share.step()), w_in.T, preferred_element_type=jnp.float32)
    gain_contribution = jnp.sum(normalized_gradient * centered_scaled_input, axis=0)
    input_gradient = normalized_gradient * layer_norm_gain
    convolution_gradient = (
        inverse_deviation
        * (
            input_gradient
            - jnp.mean(input_gradient, axis=-1, keepdims=True)
            - centered_scaled_input
            * jnp.mean(input_gradient * centered_scaled_input, axis=-1, keepdims=True)
        )
    ).astype(jnp.bfloat16)
    g_conv4 = convolution_gradient.reshape(batch, tile_h, tile_w, width)
    w_in_term = jnp.dot(normalized_input.T, g_pre, preferred_element_type=jnp.float32).astype(jnp.bfloat16)
    w_in_share = Halving(w_in_term, steps_of("dp", "row", "col"))
    g_tall = extend_along(g_conv4, "row", 1)
    first_half = kernel_gradient(padded, after(g_conv4, w_in_term), 0, 2)
    second_half = kernel_gradient(
        padded, after(g_conv4, first_half, g_tall, w_in_share.step()), 1, 2
    )
    g_padded = extend_along(g_tall, "col", 2)
    dw_term = jnp.concatenate([first_half, second_half], axis=1)
    taps = KERNEL * KERNEL
    small = jnp.concatenate([dw_term, gain_contribution[None], gamma_term[None]], axis=0)
    columns = lax.axis_size("col")
    padding = -small.shape[0] % (8 * columns)
    small = jnp.pad(small, ((0, padding), (0, 0)))
    flipped = dw_weight.reshape(KERNEL, KERNEL, width)[::-1, ::-1].reshape(KERNEL * KERNEL, width)
    images = jnp.float32(batch * lax.axis_size("dp"))
    front = batch // 2
    small = scatter_sum(small, "col")
    part = conv_back(
        after(g_padded, second_half, w_out_share.step()), flipped, out_grad, 0, front, None
    )
    w_in_second, w_out_third = w_in_share.step(), w_out_share.step()
    grad_input = conv_back(
        g_padded,
        flipped,
        out_grad,
        front,
        batch - front,
        after(part, small, w_in_second, w_out_third),
    )
    small = ordered_sum(after(small, part), "row")
    small = ordered_sum(after(small, grad_input), "dp")
    small = jnp.concatenate(collected(small, "col"), axis=0) / images
    dw_sum, gain_sum, gamma_sum = small[:taps], small[taps], small[taps + 1]
    w_out_sum, w_in_sum = w_out_share.finish(), w_in_share.finish()
    return (
        output,
        grad_input,
        w_in_sum / images,
        w_out_sum / images,
        dw_sum,
        gain_sum,
        gamma_sum,
    )


def solution(mesh):
    placed = (
        P("dp", "row", "col", None),
        P("dp"),
        P(),
        P(),
        P(),
        P(),
        P(),
        P("dp", "row", "col", None),
    )
    return jax.shard_map(
        shards,
        mesh=mesh,
        in_specs=placed,
        out_specs=(
            P("dp", "row", "col", None),
            P("dp", "row", "col", None),
            P(("dp", "row", "col"), None),
            P(("dp", "row", "col"), None),
            P(),
            P(),
            P(),
        ),
        check_vma=False,
    )
```

```python
import math

import jax
import jax.numpy as jnp
from jax import lax
from jax.experimental import pallas as pl
from jax.experimental.pallas import tpu as pltpu
from jax.sharding import PartitionSpec as P

KERNEL = 7


eps = 1e-06
keep_rate = 0.75


def extend_along(field, axis, dim, width=KERNEL // 2):
    forward = [(k, k + 1) for k in range(lax.axis_size(axis) - 1)]
    backward = [(target, source) for source, target in forward]
    full = field.shape[dim]
    low = lax.ppermute(lax.slice_in_dim(field, full - width, None, axis=dim), axis, forward)
    high = lax.ppermute(lax.slice_in_dim(field, 0, width, axis=dim), axis, backward)
    return jnp.concatenate([low, field, high], axis=dim)


def after(value, *others):
    return lax.optimization_barrier((value, *others))[0]


LANES = 128


def shifted_views(source, views, tile_w):
    wide = source[0].astype(jnp.float32)
    for j in range(KERNEL):
        views[j] = wide[:, j : j + tile_w, :]


def taps_sum(views, w_ref, top, rows, tile_w):
    acc = jnp.zeros((rows, tile_w, LANES), jnp.float32)
    for i in range(KERNEL):
        for j in range(KERNEL):
            tap = i * KERNEL + j
            acc = acc + views[j, top + i : top + i + rows] * w_ref[tap : tap + 1, :][None]
    return acc


def norm_kernel(x_ref, w_ref, gain_ref, xhat_ref, normed_ref, rstd_ref, views, held):
    step = pl.program_id(1)
    tile_h, tile_w, width = xhat_ref.shape[1:]
    shifted_views(x_ref, views, tile_w)
    half = tile_h // 2
    for top in range(0, tile_h, half):
        held[step, top : top + half] = taps_sum(views, w_ref, top, half, tile_w)

    @pl.when(step == pl.num_programs(1) - 1)
    def _():
        blocks = width // LANES

        @pl.loop(0, tile_h, step=half)
        def _(row):
            rows = pl.ds(row, half)
            total = held[0, rows]
            for block in range(1, blocks):
                total = total + held[block, rows]
            mean = jnp.sum(total, axis=-1, keepdims=True) / width
            spread = jnp.zeros_like(total)
            for block in range(blocks):
                centred = held[block, rows] - mean
                spread = spread + centred * centred
            rstd = lax.rsqrt(jnp.sum(spread, axis=-1, keepdims=True) / width + eps)
            rstd_ref[0, rows] = rstd
            for block in range(blocks):
                lanes = slice(block * LANES, (block + 1) * LANES)
                xhat = (held[block, rows] - mean) * rstd
                xhat_ref[0, rows, :, lanes] = xhat
                normed_ref[0, rows, :, lanes] = (xhat * gain_ref[:, lanes][None]).astype(jnp.bfloat16)


def conv_norm(padded, weights, gain):
    batch, full_h, full_w, width = padded.shape
    tile_h, tile_w = full_h - KERNEL + 1, full_w - KERNEL + 1
    size = batch * tile_h * tile_w * width
    shape = (batch, tile_h, tile_w, width)
    whole = pl.BlockSpec((1, tile_h, tile_w, width), lambda n, c: (n, 0, 0, 0))
    return pl.pallas_call(
        norm_kernel,
        grid=(batch, width // LANES),
        in_specs=[
            pl.BlockSpec((1, full_h, full_w, LANES), lambda n, c: (n, 0, 0, c)),
            pl.BlockSpec((KERNEL * KERNEL, LANES), lambda n, c: (0, c)),
            pl.BlockSpec((1, width), lambda n, c: (0, 0)),
        ],
        out_specs=[whole, whole, pl.BlockSpec((1, tile_h, tile_w, 1), lambda n, c: (n, 0, 0, 0))],
        out_shape=[
            jax.ShapeDtypeStruct(shape, jnp.float32),
            jax.ShapeDtypeStruct(shape, jnp.bfloat16),
            jax.ShapeDtypeStruct(shape[:3] + (1,), jnp.float32),
        ],
        scratch_shapes=[
            pltpu.VMEM((KERNEL, full_h, tile_w, LANES), jnp.float32),
            pltpu.VMEM((width // LANES, tile_h, tile_w, LANES), jnp.float32),
        ],
        compiler_params=pltpu.CompilerParams(vmem_limit_bytes=24 * 2**20),
        cost_estimate=pl.CostEstimate(flops=15000 * size, bytes_accessed=8 * size, transcendentals=0),
    )(padded, weights.astype(jnp.float32), gain[None])


def back_kernel(x_ref, w_ref, extra_ref, *rest):
    o_ref, views = rest[-2:]
    tile_h, tile_w = o_ref.shape[1], o_ref.shape[2]
    shifted_views(x_ref, views, tile_w)
    half = tile_h // 2
    for top in range(0, tile_h, half):
        acc = taps_sum(views, w_ref, top, half, tile_w)
        acc = acc + extra_ref[0, top : top + half].astype(jnp.float32)
        o_ref[0, top : top + half] = acc.astype(o_ref.dtype)


def conv_back(padded, weights, extra, start, count, earlier):
    batch, full_h, full_w, width = padded.shape
    tile_h, tile_w = full_h - KERNEL + 1, full_w - KERNEL + 1
    cell_spec = pl.BlockSpec((1, tile_h, tile_w, LANES), lambda c, n: (n + start, 0, 0, c))
    in_specs = [
        pl.BlockSpec((1, full_h, full_w, LANES), lambda c, n: (n + start, 0, 0, c)),
        pl.BlockSpec((KERNEL * KERNEL, LANES), lambda c, n: (0, c)),
        cell_spec,
    ]
    operands, aliases = [padded, weights.astype(jnp.float32), extra], {}
    if earlier is not None:
        in_specs.append(pl.BlockSpec(memory_space=pl.ANY))
        operands.append(earlier)
        aliases = {3: 0}
    size = count * tile_h * tile_w * width
    return pl.pallas_call(
        back_kernel,
        grid=(width // LANES, count),
        in_specs=in_specs,
        out_specs=cell_spec,
        out_shape=jax.ShapeDtypeStruct((batch, tile_h, tile_w, width), jnp.bfloat16),
        input_output_aliases=aliases,
        scratch_shapes=[pltpu.VMEM((KERNEL, full_h, tile_w, LANES), jnp.float32)],
        compiler_params=pltpu.CompilerParams(vmem_limit_bytes=24 * 2**20),
        cost_estimate=pl.CostEstimate(flops=15000 * size, bytes_accessed=6 * size, transcendentals=0),
    )(*operands)


def dw_kernel(x_ref, g_ref, o_ref, views, total):
    step = pl.program_id(1)
    tile_h, tile_w = g_ref.shape[1], g_ref.shape[2]
    shifted_views(x_ref, views, tile_w)

    @pl.when(step == 0)
    def _():
        total[...] = jnp.zeros_like(total)

    half = tile_h // 2
    for top in range(0, tile_h, half):
        g = g_ref[0, top : top + half].astype(jnp.float32)
        for i in range(KERNEL):
            for j in range(KERNEL):
                part = jnp.sum(views[j, top + i : top + i + half] * g, axis=0)
                part = jnp.sum(part.reshape(tile_w // 8, 8, LANES), axis=0)
                total[i * KERNEL + j] += part

    @pl.when(step == pl.num_programs(1) - 1)
    def _():
        o_ref[...] = jnp.sum(total[...], axis=1)


def kernel_gradient(padded, g_conv, part, parts):
    batch, full_h, full_w, width = padded.shape
    tile_h, tile_w = full_h - KERNEL + 1, full_w - KERNEL + 1
    blocks = width // LANES // parts
    start = blocks * part
    size = batch * tile_h * tile_w * blocks * LANES
    return pl.pallas_call(
        dw_kernel,
        grid=(blocks, batch),
        in_specs=[
            pl.BlockSpec((1, full_h, full_w, LANES), lambda c, n: (n, 0, 0, c + start)),
            pl.BlockSpec((1, tile_h, tile_w, LANES), lambda c, n: (n, 0, 0, c + start)),
        ],
        out_specs=pl.BlockSpec((KERNEL * KERNEL, LANES), lambda c, n: (0, c)),
        out_shape=jax.ShapeDtypeStruct((KERNEL * KERNEL, blocks * LANES), jnp.float32),
        scratch_shapes=[
            pltpu.VMEM((KERNEL, full_h, tile_w, LANES), jnp.float32),
            pltpu.VMEM((KERNEL * KERNEL, 8, LANES), jnp.float32),
        ],
        compiler_params=pltpu.CompilerParams(vmem_limit_bytes=24 * 2**20),
        cost_estimate=pl.CostEstimate(flops=15000 * size, bytes_accessed=6 * size, transcendentals=0),
    )(padded, g_conv)


class Halving:
    def __init__(self, term, order):
        names = ("dp", "row", "col")
        sizes = [lax.axis_size(name) for name in names]
        self.names, self.order = names, list(order)
        self.rows, self.columns = term.shape[0] // math.prod(sizes), term.shape[1]
        self.part = term.reshape(*sizes, self.rows, self.columns)
        self.done = {name: 0 for name in names}

    def step(self):
        name = self.order.pop(0)
        dim, count = self.names.index(name), lax.axis_size(name)
        stride = 2 ** self.done[name]
        self.done[name] += 1
        bit = (lax.axis_index(name) // stride) % 2
        part = self.part
        left = part.shape[dim]
        pairs = part.reshape(part.shape[:dim] + (left // 2, 2) + part.shape[dim + 1 :])
        mine = lax.dynamic_index_in_dim(pairs, bit, dim + 1, keepdims=False)
        theirs = lax.dynamic_index_in_dim(pairs, 1 - bit, dim + 1, keepdims=False)
        swap = [(k, k ^ stride) for k in range(count)]
        got = lax.ppermute(theirs.astype(jnp.bfloat16), name, swap)
        part = mine.astype(jnp.float32) + got.astype(jnp.float32)
        self.part = part.astype(jnp.bfloat16) if self.order else part
        return self.part

    def finish(self):
        while self.order:
            self.step()
        return self.part.reshape(self.rows, self.columns)


def doubled(rows, axis, bit):
    count = lax.axis_size(axis)
    return rows + lax.ppermute(rows, axis, [(k, k ^ (1 << bit)) for k in range(count)])


def steps_of(*names):
    bits = {name: int(math.log2(lax.axis_size(name))) for name in names}
    bits["col"] -= 1
    order = ["col"]
    for name in names:
        order += [name] * bits[name]
    return order


def shards(images_in, keep, dw_weight, layer_norm_gain, w_in, w_out, layer_scale, out_grad):
    batch, tile_h, tile_w, width = images_in.shape
    cells = tile_h * tile_w
    total_rows = batch * cells
    padded = extend_along(extend_along(images_in, "row", 1), "col", 2)
    xhat, normed, rstd = conv_norm(padded, dw_weight, layer_norm_gain)
    centered_scaled_input = xhat.reshape(total_rows, width)
    normalized_input = normed.reshape(total_rows, width)
    inverse_deviation = rstd.reshape(total_rows, 1)
    pre = jnp.dot(normalized_input, w_in, preferred_element_type=jnp.float32)
    cdf = 0.5 * (1.0 + lax.erf(pre * (1.0 / math.sqrt(2.0))))
    hidden = (pre * cdf).astype(jnp.bfloat16)
    branch = jnp.dot(hidden, w_out, preferred_element_type=jnp.float32)
    factor = jnp.repeat(keep.astype(jnp.float32) / keep_rate, cells)[:, None]
    flat_in = images_in.reshape(total_rows, width).astype(jnp.float32)
    output = (flat_in + factor * layer_scale * branch).astype(jnp.bfloat16).reshape(images_in.shape)
    upstream = out_grad.reshape(total_rows, width).astype(jnp.float32)
    g_branch = (factor * layer_scale * upstream).astype(jnp.bfloat16)
    w_out_term = jnp.dot(hidden.T, g_branch, preferred_element_type=jnp.float32).astype(jnp.bfloat16)
    w_out_share = Halving(w_out_term, steps_of("col", "row", "dp"))
    gamma_term = jnp.sum(factor * upstream * branch, axis=0)
    slope = cdf + pre * jnp.exp(-0.5 * pre * pre) * (1.0 / math.sqrt(2.0 * math.pi))
    g_pre = (jnp.dot(after(g_branch, w_out_term), w_out.T, preferred_element_type=jnp.float32) * slope).astype(
        jnp.bfloat16
    )
    normalized_gradient = jnp.dot(after(g_pre, w_out_share.step()), w_in.T, preferred_element_type=jnp.float32)
    gain_contribution = jnp.sum(normalized_gradient * centered_scaled_input, axis=0)
    input_gradient = normalized_gradient * layer_norm_gain
    convolution_gradient = (
        inverse_deviation
        * (
            input_gradient
            - jnp.mean(input_gradient, axis=-1, keepdims=True)
            - centered_scaled_input
            * jnp.mean(input_gradient * centered_scaled_input, axis=-1, keepdims=True)
        )
    ).astype(jnp.bfloat16)
    g_conv4 = convolution_gradient.reshape(batch, tile_h, tile_w, width)
    w_in_term = jnp.dot(normalized_input.T, g_pre, preferred_element_type=jnp.float32).astype(jnp.bfloat16)
    w_in_share = Halving(w_in_term, steps_of("dp", "col", "row"))
    g_tall = extend_along(g_conv4, "row", 1)
    first_half = kernel_gradient(padded, after(g_conv4, w_in_term), 0, 2)
    w_in_share.part = after(w_in_share.step(), first_half)
    second_half = kernel_gradient(
        padded, after(g_conv4, first_half, g_tall, w_in_share.part, w_out_share.step()), 1, 2
    )
    g_padded = extend_along(g_tall, "col", 2)
    dw_term = jnp.concatenate([first_half, second_half], axis=1)
    taps = KERNEL * KERNEL
    small = jnp.concatenate([dw_term, gain_contribution[None], gamma_term[None]], axis=0)
    bits = [
        (axis, bit)
        for axis in ("col", "dp", "row")
        for bit in range(int(math.log2(lax.axis_size(axis))))
    ]
    flipped = dw_weight.reshape(KERNEL, KERNEL, width)[::-1, ::-1].reshape(KERNEL * KERNEL, width)
    images = jnp.float32(batch * lax.axis_size("dp"))
    front = batch // 2
    small = doubled(small, *bits[0])
    part = conv_back(
        after(g_padded, second_half, w_in_share.step(), small),
        flipped,
        out_grad,
        0,
        front,
        None,
    )
    small = doubled(small, *bits[1])
    grad_input = conv_back(
        g_padded,
        flipped,
        out_grad,
        front,
        batch - front,
        after(part, small, w_in_share.step(), w_out_share.step()),
    )
    small = doubled(after(small, part), *bits[2])
    small = after(small, grad_input)
    for axis, bit in bits[3:]:
        small = doubled(small, axis, bit)
    small = small / images
    dw_sum, gain_sum, gamma_sum = small[:taps], small[taps], small[taps + 1]
    w_out_sum, w_in_sum = w_out_share.finish(), w_in_share.finish()
    return (
        output,
        grad_input,
        w_in_sum / images,
        w_out_sum / images,
        dw_sum,
        gain_sum,
        gamma_sum,
    )


def solution(mesh):
    placed = (
        P("dp", "row", "col", None),
        P("dp"),
        P(),
        P(),
        P(),
        P(),
        P(),
        P("dp", "row", "col", None),
    )
    return jax.shard_map(
        shards,
        mesh=mesh,
        in_specs=placed,
        out_specs=(
            P("dp", "row", "col", None),
            P("dp", "row", "col", None),
            P(("dp", "row", "col"), None),
            P(("dp", "row", "col"), None),
            P(),
            P(),
            P(),
        ),
        check_vma=False,
    )
```
